128 devices in a mesh: ctx: 16 (over z, x), tp: 8 (over y, core).
Axes of the slice: x: 4, y: 4, z: 4, core: 2. Of those that a mesh axis runs over, the one named last changes fastest.
Arguments:
- queries: bfloat16 [16384, 8192], P('ctx', 'tp'), may hold values from -6 to 6
- key_proj: bfloat16 [16384, 8192], P('ctx', 'tp'), may hold values from -6 to 6
- values: bfloat16 [16384, 8192], P('ctx', 'tp'), may hold values from -6 to 6
- gate_input: bfloat16 [16384, 8192], P('ctx', 'tp'), may hold values from -8 to 8
- norm_gain: float32 [8192], P('tp'), may hold values from 0.1 to 1.9
- out_weight: bfloat16 [8192, 6144], P('tp'), may hold values from -0.0625 to 0.0625
Outputs:
- layer_out: bfloat16 [16384, 6144], P('ctx', 'tp')
The draws below stay inside these ranges and needn't reach their ends.
All inputs are finite; a program needn't handle non-finite values.
Results may differ from the reference program's by a relative error of at most 0.02.
Values may be sent and summed in bfloat16 or wider, within the bound.
No kernel may reach another device: no remote copies, remote signals or barrier semaphores. Data moves between devices by JAX's collectives and lax.ppermute only.
A program may use at most 128 MiB of HBM per device.

```python
import jax
import jax.numpy as jnp
from jax import lax

D = 6144
HEADS = 64
DH = 128
TOK_DEV = 1024
TOKENS = 16384
HD = 8192
N_CTX = 16
N_TP = 8


def level_of(own_key, shape, split, low, largest):
    gain, own = 1.0, jax.random.fold_in(own_key, 6)
    for axis_at, blocks in split:
        heights = jnp.exp(jax.random.uniform(jax.random.fold_in(own, axis_at), (blocks,), jnp.float32, low / len(split), largest / len(split)))
        gain = gain * jnp.repeat(heights, shape[axis_at] // blocks).reshape([-1 if axis == axis_at else 1 for axis in range(len(shape))])
    return gain


def gaussian(own_key, shape, width, limit, split=(), held_as=jnp.bfloat16):
    drawn = jax.random.normal(own_key, shape, jnp.float32) * width
    if len(split) > 0:
        drawn = level_of(own_key, shape, split, -0.22, 0.18) * drawn
    return jnp.clip(drawn, min=-limit, max=limit).astype(held_as)


def setup_inputs(seed: int = 0) -> dict:
    seeds = jax.random.split(jax.random.key(seed), 7)
    queries = gaussian(seeds[0], (TOKENS, HD), 1.0, 6.0, ((0, 16), (1, 8)))
    key_proj = gaussian(seeds[1], (TOKENS, HD), 1.0, 6.0, ((0, 16), (1, 8)))
    values = gaussian(seeds[2], (TOKENS, HD), 1.0, 6.0, ((0, 16), (1, 8)))
    gate_input = gaussian(seeds[3], (TOKENS, HD), 1.5, 8.0, ((0, 16), (1, 8)))
    norm_gain = jnp.clip(1.0 + 0.18 * jax.random.normal(seeds[4], (HD,), jnp.float32), 0.1, 1.9)
    out_weight = gaussian(seeds[5], (HD, D), HD ** -0.5, 0.0625, ((0, 8),))
    return {"queries": queries, "key_proj": key_proj, "values": values, "gate_input": gate_input, "norm_gain": norm_gain, "out_weight": out_weight}


def reference(queries, key_proj, values, gate_input, norm_gain, out_weight):
    qfeat = jax.nn.silu(queries.astype(jnp.float32)).astype(jnp.bfloat16)
    kfeat = jax.nn.silu(key_proj.astype(jnp.float32)).astype(jnp.bfloat16)
    qblocks = qfeat.reshape(N_CTX, TOK_DEV, HEADS, DH)
    kblocks = kfeat.reshape(N_CTX, TOK_DEV, HEADS, DH)
    vblocks = values.reshape(N_CTX, TOK_DEV, HEADS, DH)
    causal = jnp.arange(TOK_DEV)[:, None] >= jnp.arange(TOK_DEV)[None, :]

    def block_step(state, inputs):
        qblk, kblk, vblk = inputs
        qf = qblk.astype(jnp.float32)
        kf = kblk.astype(jnp.float32)
        vf = vblk.astype(jnp.float32)
        scores = jnp.einsum('thd,shd->hts', qf, kf)
        scores = jnp.where(causal[None], scores, 0.0).astype(jnp.bfloat16)
        intra = jnp.einsum('hts,she->the', scores.astype(jnp.float32), vf)
        inter = jnp.einsum('thd,hde->the', qf, state, precision=lax.Precision.HIGHEST)
        local = jnp.einsum('thd,the->hde', kf, vf)
        return (state + local, intra + inter)
    start = jnp.zeros((HEADS, DH, DH), jnp.float32)
    final_state, attn = lax.scan(block_step, start, (qblocks, kblocks, vblocks))
    attn = attn.reshape(TOKENS, HEADS, DH)
    meansq = lax.optimization_barrier(jnp.mean(attn * attn, axis=-1, keepdims=True))
    normed = (attn / jnp.sqrt(meansq + 1e-06)).reshape(TOKENS, HD)
    hidden = (normed * norm_gain[None, :] * jax.nn.sigmoid(gate_input.astype(jnp.float32))).astype(jnp.bfloat16)
    group_width = HD // N_TP
    hidden_groups = hidden.reshape(TOKENS, N_TP, group_width).transpose(1, 0, 2)
    weight_groups = out_weight.reshape(N_TP, group_width, D)

    def group_step(total, inputs):
        hgroup, wgroup = inputs
        partial_value = jnp.dot(hgroup, wgroup, preferred_element_type=jnp.float32).astype(jnp.bfloat16)
        partial_value = lax.optimization_barrier(partial_value)
        return (total + partial_value.astype(jnp.float32), None)
    total, unused = lax.scan(group_step, jnp.zeros((TOKENS, D), jnp.float32), (hidden_groups, weight_groups))
    return total.astype(jnp.bfloat16)
```

```python
import functools

import jax
import jax.numpy as jnp
from jax import lax
from jax.experimental import pallas as pl
from jax.experimental.pallas import tpu as pltpu
from jax.sharding import PartitionSpec as P

DH = 128
N_X = 4
N_Z = 4
N_Y = 4
CHUNK = 256
F32 = jnp.float32
BF16 = jnp.bfloat16
ROW_BLOCK = 128


def shift_x(k):
    return [(z * N_X + x, z * N_X + (x + k) % N_X) for z in range(N_Z) for x in range(N_X)]


def later_z(k):
    return [(z * N_X + x, (z + k) * N_X + x) for z in range(N_Z - k) for x in range(N_X)]


def shift_y(k):
    return [(y * 2 + c, ((y + k) % N_Y) * 2 + c) for y in range(N_Y) for c in range(2)]


OTHER_CORE = [(i, i ^ 1) for i in range(2 * N_Y)]


def sigmoid(x):
    return 0.5 * jnp.tanh(0.5 * x) + 0.5


def feature(x):
    wide = x.astype(F32)
    return (wide * sigmoid(wide)).astype(BF16)


def call(kernel, vmem=24, **kwargs):
    compiler_params = pltpu.CompilerParams(vmem_limit_bytes=vmem << 20)
    cost = pl.CostEstimate(flops=1, bytes_accessed=1, transcendentals=0)
    return pl.pallas_call(kernel, compiler_params=compiler_params, cost_estimate=cost, **kwargs)


def in_hbm(x):
    return pltpu.with_memory_space_constraint(x, pltpu.HBM)


def in_vmem(x):
    return pltpu.with_memory_space_constraint(x, pltpu.VMEM)


def state_kernel(k_ref, v_ref, state_ref):
    for h in range(k_ref.shape[1] // DH):
        cols = slice(h * DH, (h + 1) * DH)
        kf = feature(k_ref[:, cols])
        state = lax.dot_general(kf, v_ref[:, cols], (((0,), (0,)), ((), ())), preferred_element_type=F32)
        state_ref[cols, :] = state.astype(BF16)


def local_states(keys, values):
    rows, width = keys.shape
    block = 2 * DH
    spec = pl.BlockSpec((rows, block), lambda i: (0, i))
    return call(
        state_kernel,
        name="local_states",
        grid=(width // block,),
        in_specs=[spec, spec],
        out_specs=pl.BlockSpec((block, DH), lambda i: (i, 0)),
        out_shape=jax.ShapeDtypeStruct((width, DH), BF16),
    )(in_hbm(keys), in_hbm(values))


def split(x):
    high = x.astype(BF16)
    return high, (x - high.astype(F32)).astype(BF16)


def two_part_dot(q, high, low):
    return jnp.dot(
        jnp.concatenate([q, q], axis=1), jnp.concatenate([high, low], axis=0), preferred_element_type=F32
    )


def intra_kernel(q_ref, k_ref, v_ref, after_ref, intra_ref, qfeat_ref):
    rows = q_ref.shape[0]
    t = lax.broadcasted_iota(jnp.int32, (CHUNK, CHUNK), 0)
    s = lax.broadcasted_iota(jnp.int32, (CHUNK, CHUNK), 1)
    causal = s <= t
    for h in range(q_ref.shape[1] // DH):
        cols = slice(h * DH, (h + 1) * DH)
        state = jnp.zeros((DH, DH), F32)
        for i in range(rows // CHUNK):
            here = slice(i * CHUNK, (i + 1) * CHUNK)
            q, k, v = feature(q_ref[here, cols]), feature(k_ref[here, cols]), v_ref[here, cols]
            qfeat_ref[here, cols] = q
            scores = lax.dot_general(q, k, (((1,), (1,)), ((), ())), preferred_element_type=F32)
            scores = jnp.where(causal, scores, 0.0).astype(BF16)
            out = jnp.dot(scores, v, preferred_element_type=F32)
            if i:
                out += two_part_dot(q, *split(state))
            intra_ref[here, cols] = out
            if (i + 1) * CHUNK < rows:
                state += lax.dot_general(k, v, (((0,), (0,)), ((), ())), preferred_element_type=F32)


def intra_block(queries, keys, values, after):
    rows, width = keys.shape
    block = 2 * DH
    spec = pl.BlockSpec((rows, block), lambda i: (0, i))
    return call(
        intra_kernel,
        name="intra_block",
        grid=(width // block,),
        in_specs=[spec] * 3 + [pl.BlockSpec(memory_space=pl.ANY)],
        out_specs=[spec] * 2,
        out_shape=[
            pltpu.VMEM((rows, width), F32),
            pltpu.VMEM((rows, width), BF16),
        ],
    )(in_hbm(queries), in_hbm(keys), in_hbm(values), *after)


def hidden_kernel(n_parts, *refs):
    intra_ref, qfeat_ref, gate_ref, gain_ref = refs[:4]
    part_refs, hidden_ref, both_ref = refs[4 : 4 + n_parts], refs[-2], refs[-1]
    width = intra_ref.shape[1]

    @pl.when(pl.program_id(0) == 0)
    def _():
        prefix = part_refs[0][...].astype(F32)
        for ref in part_refs[1:]:
            prefix += ref[...].astype(F32)
        high, low = split(prefix)
        for h in range(width // DH):
            both_ref[h, :DH, :] = high[h * DH : (h + 1) * DH]
            both_ref[h, DH:, :] = low[h * DH : (h + 1) * DH]

    for h in range(width // DH):
        cols = slice(h * DH, (h + 1) * DH)
        q = qfeat_ref[:, cols]
        inter = jnp.dot(jnp.concatenate([q, q], axis=1), both_ref[h], preferred_element_type=F32)
        attn = intra_ref[:, cols] + inter
        scale = lax.rsqrt(jnp.mean(attn * attn, axis=-1, keepdims=True) + 1e-06)
        gate = sigmoid(gate_ref[:, cols].astype(F32))
        hidden_ref[:, cols] = (attn * scale * gain_ref[:, cols] * gate).astype(BF16)


def hidden_rows(part, intra, qfeat, gate_input, gain, parts, after):
    rows, width = intra.shape
    steps = rows // 2 // ROW_BLOCK
    spec = pl.BlockSpec((ROW_BLOCK, width), lambda i: (i // (steps // 2) * steps + part * (steps // 2) + i % (steps // 2), 0))
    return call(
        functools.partial(hidden_kernel, len(parts)),
        name="hidden_rows",
        grid=(steps,),
        in_specs=[spec, spec, spec, pl.BlockSpec((1, width), lambda i: (0, 0))]
        + [pl.BlockSpec((width, DH), lambda i: (0, 0))] * len(parts)
        + [pl.BlockSpec(memory_space=pl.ANY)] * len(after),
        out_specs=pl.BlockSpec((ROW_BLOCK, width), lambda i: (i, 0)),
        out_shape=pltpu.VMEM((rows // 2, width), BF16),
        scratch_shapes=[pltpu.VMEM((width // DH, 2 * DH, DH), BF16)],
    )(in_vmem(intra), in_vmem(qfeat), in_vmem(gate_input), gain, *parts, *after)


def project_kernel(plan, n_hidden, n_adds, n_outs, n_after, blocks_ref, *refs):
    own, other = refs[:n_hidden], refs[n_hidden : 2 * n_hidden]
    w_own, w_other = refs[2 * n_hidden : 2 * n_hidden + 2]
    adds = refs[2 * n_hidden + 2 : 2 * n_hidden + 2 + n_adds]
    outs = refs[len(refs) - n_outs :]
    steps = w_own.shape[1]
    for group, pieces in enumerate(plan):

        def work(pieces=pieces):
            cols = pl.ds(pl.multiple_of(lax.rem(pl.program_id(0), 3) * steps, steps), steps)
            for source, first, rows, terms, out, at in pieces:
                here = slice(first, first + rows)
                value = jnp.dot(own[source][here, :], w_own[...], preferred_element_type=F32)
                value += jnp.dot(other[source][here, :], w_other[...], preferred_element_type=F32)
                for term, term_first in terms:
                    value += adds[term][term_first : term_first + rows, cols].astype(F32)
                outs[out][at : at + rows, cols] = value.astype(outs[out].dtype)

        pl.when(pl.program_id(0) // 3 == group)(work)


def project(name, own, other, w_own, w_other, blocks, plan, outs, adds=(), after=()):
    third = w_own.shape[1] // (2 * N_Y) // 3
    depth = w_own.shape[0]
    whole = lambda a: pl.BlockSpec(memory_space=pltpu.VMEM)
    w_spec = pl.BlockSpec((depth, third), lambda i, b: (0, b[i // 3] * 3 + lax.rem(i, 3)))
    return call(
        functools.partial(project_kernel, plan, len(own), len(adds), len(outs), len(after)),
        name=name,
        grid_spec=pltpu.PrefetchScalarGridSpec(
            num_scalar_prefetch=1,
            grid=(3 * len(plan),),
            in_specs=[whole(h) for h in own]
            + [whole(h) for h in other]
            + [w_spec, w_spec]
            + [whole(a) for a in adds]
            + [pl.BlockSpec(memory_space=pl.ANY)] * len(after),
            out_specs=[pl.BlockSpec(memory_space=pltpu.VMEM) for _ in outs],
        ),
        out_shape=[pltpu.VMEM((n, 3 * third), dtype) for n, dtype in outs],
    )(blocks, *map(in_vmem, own + other), in_hbm(w_own), in_hbm(w_other), *map(in_vmem, adds), *after)


def finish_kernel(top_ref, bottom_ref, top_add_ref, bottom_add_ref, out_ref):
    half = top_ref.shape[0]
    out_ref[:half, :] = (top_ref[...] + top_add_ref[...].astype(F32)).astype(BF16)
    out_ref[half:, :] = (bottom_ref[...] + bottom_add_ref[...].astype(F32)).astype(BF16)


def finish(*halves):
    rows, width = halves[0].shape
    block = width // 2
    return call(
        finish_kernel,
        name="finish",
        grid=(2,),
        in_specs=[pl.BlockSpec((rows, block), lambda i: (0, i))] * 4,
        out_specs=pl.BlockSpec((2 * rows, block), lambda i: (0, i)),
        out_shape=jax.ShapeDtypeStruct((2 * rows, width), BF16),
    )(*map(in_vmem, halves))


def on_device(queries, key_proj, values, gate_input, norm_gain, out_weight):
    rows, width = queries.shape
    half, quarter = rows // 2, rows // 4
    x = lax.rem(lax.axis_index("ctx"), N_X)
    y, core = lax.axis_index("tp") // 2, lax.rem(lax.axis_index("tp"), 2)
    gain = norm_gain[None, :]
    blocks = [((y + k) % N_Y * 2 + core).astype(jnp.int32) for k in range(N_Y)]

    other_weight = lax.ppermute(out_weight, "tp", OTHER_CORE)
    state = local_states(key_proj, values)
    along_x = [lax.ppermute(state, "ctx", shift_x(k)) for k in (1, 3, 2)]
    intra, qfeat = intra_block(queries, key_proj, values, [state])
    total = state.astype(F32)
    earlier = jnp.zeros_like(total)
    for k, part in zip((1, 3, 2), along_x):
        wide = part.astype(F32)
        total += wide
        earlier += jnp.where(k <= x, wide, 0.0)
    total = total.astype(BF16)
    along_z = [lax.ppermute(total, "ctx", later_z(k)) for k in (1, 2, 3)]
    parts = [earlier, *along_z]

    swap = lambda a: lax.ppermute(a, "tp", OTHER_CORE)
    up = lambda a: lax.ppermute(a, "tp", shift_y(1))
    down = lambda a: lax.ppermute(a, "tp", shift_y(-1))
    own = [hidden_rows(0, intra, qfeat, gate_input, gain, parts, [])]
    own.append(hidden_rows(1, intra, qfeat, gate_input, gain, parts, own))
    other = [swap(own[0]), swap(own[1])]

    far = (((0, 0, quarter, (), 0, 0), (0, quarter, quarter, (), 1, 0)),)
    far_up, far_down, last = [], [], own[1]
    for i in range(2):
        top, bottom = project(
            "share_far", own[i : i + 1], other[i : i + 1], out_weight, other_weight, blocks[2][None],
            far, [(quarter, BF16)] * 2, after=[last],
        )
        far_up.append(up(top))
        far_down.append(down(bottom))
        last = top

    near_blocks = jnp.stack([blocks[1], blocks[3]])
    near = tuple(
        tuple((i, part * quarter, quarter, (), g, i * quarter) for i in range(2)) for g, part in ((0, 1), (1, 0))
    )
    up_share, down_share = project(
        "share_near", own, other, out_weight, other_weight, near_blocks, near, [(half, BF16)] * 2,
        after=[last, far_up[0], far_down[0]],
    )
    bottom_from_below, top_from_above = up(up_share), down(down_share)

    passing = tuple(
        tuple((i, part * quarter, quarter, ((2 * g + i, 0),), g, i * quarter) for i in range(2))
        for g, part in ((0, 0), (1, 1))
    )
    up_sum, down_sum = project(
        "share_passing", own, other, out_weight, other_weight, near_blocks, passing, [(half, BF16)] * 2,
        adds=[*far_up, *far_down], after=[up_share],
    )
    top_from_below, bottom_from_above = up(up_sum), down(down_sum)

    mine = (
        tuple(
            (i, part * quarter, quarter, ((part, i * quarter),), part, i * quarter) for part in range(2) for i in range(2)
        ),
    )
    top, bottom = project(
        "share_own", own, other, out_weight, other_weight, blocks[0][None], mine, [(half, F32)] * 2,
        adds=[top_from_above, bottom_from_below], after=[up_sum],
    )
    return finish(top, bottom, top_from_below, bottom_from_above)


def solution(mesh):
    return jax.shard_map(
        on_device,
        mesh=mesh,
        in_specs=(
            P("ctx", "tp"),
            P("ctx", "tp"),
            P("ctx", "tp"),
            P("ctx", "tp"),
            P("tp"),
            P("tp", None),
        ),
        out_specs=P("ctx", "tp"),
        check_vma=False,
    )
```

```python
import functools

import jax
import jax.numpy as jnp
from jax import lax
from jax.experimental import pallas as pl
from jax.experimental.pallas import tpu as pltpu
from jax.sharding import PartitionSpec as P

DH = 128
N_X = 4
N_Z = 4
N_Y = 4
CHUNK = 256
F32 = jnp.float32
BF16 = jnp.bfloat16
FAR_ROWS = (256, 256)
PADDING = (0, 0)
BLOCK_ORDER = (2, 1, 3, 0)


def shift_x(k):
    return [(z * N_X + x, z * N_X + (x + k) % N_X) for z in range(N_Z) for x in range(N_X)]


def later_z(k):
    return [(z * N_X + x, (z + k) * N_X + x) for z in range(N_Z - k) for x in range(N_X)]


def shift_y(k):
    return [(y * 2 + c, ((y + k) % N_Y) * 2 + c) for y in range(N_Y) for c in range(2)]


OTHER_CORE = [(i, i ^ 1) for i in range(2 * N_Y)]


def sigmoid(x):
    return 0.5 * jnp.tanh(0.5 * x) + 0.5


def feature(x):
    wide = x.astype(F32)
    return (wide * sigmoid(wide)).astype(BF16)


def call(kernel, vmem=16, flops=1, **kwargs):
    compiler_params = pltpu.CompilerParams(vmem_limit_bytes=vmem << 20)
    cost = pl.CostEstimate(flops=flops, bytes_accessed=1, transcendentals=0)
    return pl.pallas_call(kernel, compiler_params=compiler_params, cost_estimate=cost, **kwargs)


def in_hbm(x):
    return pltpu.with_memory_space_constraint(x, pltpu.HBM)


def in_vmem(x):
    return pltpu.with_memory_space_constraint(x, pltpu.VMEM)


IN_VMEM = pl.BlockSpec(memory_space=pltpu.VMEM)
ANYWHERE = pl.BlockSpec(memory_space=pl.ANY)


def state_kernel(k_ref, v_ref, state_ref):
    for h in range(k_ref.shape[1] // DH):
        cols = slice(h * DH, (h + 1) * DH)
        kf = feature(k_ref[:, cols])
        state = lax.dot_general(kf, v_ref[:, cols], (((0,), (0,)), ((), ())), preferred_element_type=F32)
        state_ref[cols, :] = state.astype(BF16)


def local_states(keys, values):
    rows, width = keys.shape
    block = 2 * DH
    spec = pl.BlockSpec((rows, block), lambda i: (0, i))
    return call(
        state_kernel,
        name="local_states",
        grid=(width // block,),
        in_specs=[spec, spec],
        out_specs=pl.BlockSpec((block, DH), lambda i: (i, 0)),
        out_shape=jax.ShapeDtypeStruct((width, DH), BF16),
    )(in_hbm(keys), in_hbm(values))


def split(x):
    high = x.astype(BF16)
    return high, (x - high.astype(F32)).astype(BF16)


def two_part_dot(q, high, low):
    return jnp.dot(
        jnp.concatenate([q, q], axis=1), jnp.concatenate([high, low], axis=0), preferred_element_type=F32
    )


def intra_kernel(q_ref, k_ref, v_ref, after_ref, intra_ref, qfeat_ref):
    rows, block = q_ref.shape
    t = lax.broadcasted_iota(jnp.int32, (CHUNK, CHUNK), 0)
    s = lax.broadcasted_iota(jnp.int32, (CHUNK, CHUNK), 1)
    causal = s <= t
    for h in range(q_ref.shape[1] // DH):
        cols = slice(h * DH, (h + 1) * DH)
        out_cols = pl.ds(pl.multiple_of(pl.program_id(0) * block + h * DH, DH), DH)
        state = jnp.zeros((DH, DH), F32)
        for i in range(rows // CHUNK):
            here = slice(i * CHUNK, (i + 1) * CHUNK)
            q, k, v = feature(q_ref[here, cols]), feature(k_ref[here, cols]), v_ref[here, cols]
            qfeat_ref[here, out_cols] = q
            scores = lax.dot_general(q, k, (((1,), (1,)), ((), ())), preferred_element_type=F32)
            scores = jnp.where(causal, scores, 0.0).astype(BF16)
            out = jnp.dot(scores, v, preferred_element_type=F32)
            if i:
                out += two_part_dot(q, *split(state))
            intra_ref[here, out_cols] = out
            if (i + 1) * CHUNK < rows:
                state += lax.dot_general(k, v, (((0,), (0,)), ((), ())), preferred_element_type=F32)


def intra_block(queries, keys, values, after):
    rows, width = keys.shape
    block = 2 * DH
    spec = pl.BlockSpec((rows, block), lambda i: (0, i))
    return call(
        intra_kernel,
        name="intra_block",
        flops=10**11,
        grid=(width // block,),
        in_specs=[spec] * 3 + [ANYWHERE],
        out_specs=[IN_VMEM] * 2,
        out_shape=[
            pltpu.VMEM((rows, width), F32),
            pltpu.VMEM((rows, width), BF16),
        ],
    )(in_hbm(queries), in_hbm(keys), in_hbm(values), *after)


def sort_columns_kernel(blocks_ref, weight_ref, after_ref, far_ref, rest_ref, mine_ref):
    step = pl.program_id(0)

    @pl.when(step == 0)
    def _():
        far_ref[0] = weight_ref[...]

    @pl.when((step > 0) & (step < N_Y))
    def _():
        rest_ref[0] = weight_ref[...]

    @pl.when(step >= N_Y)
    def _():
        mine_ref[0] = weight_ref[...]


def sort_columns(weight, theirs, mine, after):
    rows, width = weight.shape
    block = (rows, width // (2 * N_Y))
    return call(
        sort_columns_kernel,
        vmem=24,
        name="sort_columns",
        grid_spec=pltpu.PrefetchScalarGridSpec(
            num_scalar_prefetch=1,
            grid=(2 * N_Y,),
            in_specs=[pl.BlockSpec(block, lambda i, b: (0, b[i])), ANYWHERE],
            out_specs=[
                pl.BlockSpec((1, *block), lambda i, b: (0, 0, 0)),
                pl.BlockSpec((1, *block), lambda i, b: (jnp.clip(i - 1, 0, N_Y - 2), 0, 0)),
                pl.BlockSpec((1, *block), lambda i, b: (jnp.maximum(i - N_Y, 0), 0, 0)),
            ],
        ),
        out_shape=[pltpu.HBM((n, *block), BF16) for n in (1, N_Y - 1, N_Y)],
    )(jnp.stack(theirs + mine), in_hbm(weight), *after)


def pass_kernel(*refs):
    pass


def settled(arrays, after):
    return call(
        pass_kernel,
        name="settled",
        in_specs=[IN_VMEM] * len(arrays) + [ANYWHERE] * len(after),
        out_specs=[IN_VMEM] * len(arrays),
        out_shape=[pltpu.VMEM(a.shape, a.dtype) for a in arrays],
        input_output_aliases={i: i for i in range(len(arrays))},
    )(*map(in_vmem, arrays), *after)


def hidden_kernel(n_parts, first, rows, *refs):
    intra_ref, qfeat_ref, gate_ref, gain_ref = refs[:4]
    part_refs, hidden_ref, both_ref = refs[4 : 4 + n_parts], refs[-2], refs[-1]
    tokens, width = intra_ref.shape

    prefix = part_refs[0][...].astype(F32)
    for ref in part_refs[1:]:
        prefix += ref[...].astype(F32)
    high, low = split(prefix)
    for h in range(width // DH):
        both_ref[h, :DH, :] = high[h * DH : (h + 1) * DH]
        both_ref[h, DH:, :] = low[h * DH : (h + 1) * DH]

    for part in range(2):
        here = slice(part * tokens // 2 + first, part * tokens // 2 + first + rows)
        there = slice(part * rows, (part + 1) * rows)
        for h in range(width // DH):
            cols = slice(h * DH, (h + 1) * DH)
            q = qfeat_ref[here, cols]
            inter = jnp.dot(jnp.concatenate([q, q], axis=1), both_ref[h], preferred_element_type=F32)
            attn = intra_ref[here, cols] + inter
            scale = lax.rsqrt(jnp.mean(attn * attn, axis=-1, keepdims=True) + 1e-06)
            gate = sigmoid(gate_ref[here, cols].astype(F32))
            hidden_ref[there, cols] = (attn * scale * gain_ref[:, cols] * gate).astype(BF16)


def hidden_rows(first, rows, intra, qfeat, gate_input, gain, parts, after):
    width = intra.shape[1]
    return call(
        functools.partial(hidden_kernel, len(parts), first, rows),
        name="hidden_rows",
        in_specs=[IN_VMEM] * (4 + len(parts)) + [ANYWHERE] * len(after),
        out_specs=IN_VMEM,
        out_shape=pltpu.VMEM((2 * rows, width), BF16),
        scratch_shapes=[pltpu.VMEM((width // DH, 2 * DH, DH), BF16)],
    )(*map(in_vmem, [intra, qfeat, gate_input, gain, *parts]), *after)


def project_kernel(blocks, plan, n_hidden, n_adds, n_outs, *refs):
    own, other = refs[:n_hidden], refs[n_hidden : 2 * n_hidden]
    w_own, w_other = refs[2 * n_hidden : 2 * n_hidden + 2]
    adds = refs[2 * n_hidden + 2 :][:n_adds]
    outs = refs[len(refs) - n_outs :]
    step = outs[0].shape[1] // 3
    ends = [max(piece[5] + piece[2] for pieces in plan for piece in pieces if piece[4] == out) for out in range(n_outs)]
    for (mine, theirs), pieces in zip(blocks, plan):
        for source, first, rows, terms, out, at in pieces:

            def third(i, _, mine=mine, theirs=theirs, source=source, first=first, rows=rows, terms=terms, out=out, at=at):
                cols = pl.ds(pl.multiple_of(i * step, step), step)
                here = slice(first, first + rows)
                value = jnp.dot(own[source][here, :], w_own[mine, :, cols], preferred_element_type=F32)
                value += jnp.dot(other[source][here, :], w_other[theirs, :, cols], preferred_element_type=F32)
                for term, term_first in terms:
                    value += adds[term][term_first : term_first + rows, cols].astype(F32)
                outs[out][at : at + rows, cols] = value.astype(outs[out].dtype)
                return 0

            lax.fori_loop(0, 3, third, 0)
    for out, end in zip(outs, ends):
        if end < out.shape[0]:
            out[end:, :] = jnp.zeros((out.shape[0] - end, out.shape[1]), out.dtype)


def project(name, own, other, w_own, w_other, blocks, plan, outs, adds=(), after=(), flops=1):
    width = w_own.shape[2]
    operands = [*own, *other, w_own, w_other, *adds]
    return call(
        functools.partial(project_kernel, blocks, plan, len(own), len(adds), len(outs)),
        name=name,
        flops=flops,
        in_specs=[IN_VMEM] * len(operands) + [ANYWHERE] * len(after),
        out_specs=[IN_VMEM] * len(outs),
        out_shape=[pltpu.VMEM((n, width), dtype) for n, dtype in outs],
    )(*map(in_vmem, operands), *after)


def finish_kernel(*refs):
    values, adds, out_ref = refs[:2], refs[2:4], refs[4]
    rows = out_ref.shape[0]
    step = pl.program_id(0)
    steps = values[0].shape[0] // rows
    here = pl.ds(pl.multiple_of(lax.rem(step, steps) * rows, rows), rows)
    for value, add, half in zip(values, adds, range(2)):

        @pl.when(step // steps == half)
        def _(value=value, add=add):
            out_ref[...] = (value[here, :] + add[here, :].astype(F32)).astype(BF16)


def finish(*halves):
    rows, width = halves[0].shape
    block = rows // 2
    return call(
        finish_kernel,
        name="finish",
        grid=(2 * rows // block,),
        in_specs=[IN_VMEM] * 4,
        out_specs=pl.BlockSpec((block, width), lambda i: (i, 0)),
        out_shape=jax.ShapeDtypeStruct((2 * rows, width), BF16),
    )(*map(in_vmem, halves))


def on_device(queries, key_proj, values, gate_input, norm_gain, out_weight):
    rows, width = queries.shape
    half = rows // 2
    firsts = (0, FAR_ROWS[0])
    x = lax.rem(lax.axis_index("ctx"), N_X)
    y, core = lax.axis_index("tp") // 2, lax.rem(lax.axis_index("tp"), 2)
    gain = norm_gain[None, :]
    mine = [((y + k) % N_Y * 2 + core).astype(jnp.int32) for k in BLOCK_ORDER]
    theirs = [((y + k) % N_Y * 2 + 1 - core).astype(jnp.int32) for k in BLOCK_ORDER]

    state = local_states(key_proj, values)
    along_x = [lax.ppermute(state, "ctx", shift_x(k)) for k in (2, 3, 1)]
    theirs_far, theirs_rest, own_weight = sort_columns(out_weight, theirs, mine, [state])
    swap = lambda a: lax.ppermute(a, "tp", OTHER_CORE)
    other_far, other_rest = swap(theirs_far), swap(theirs_rest)
    state, own_weight = lax.optimization_barrier((state, own_weight))
    intra, qfeat = intra_block(queries, key_proj, values, [state])
    total = state.astype(F32)
    earlier = jnp.zeros_like(total)
    for k, part in zip((2, 3, 1), along_x):
        wide = part.astype(F32)
        total += wide
        earlier += jnp.where(k <= x, wide, 0.0)
    total = total.astype(BF16)
    along_z = [lax.ppermute(total, "ctx", later_z(k)) for k in (2, 3, 1)]
    parts = [earlier, *along_z]

    up = lambda a: lax.ppermute(a, "tp", shift_y(1))
    down = lambda a: lax.ppermute(a, "tp", shift_y(-1))
    own = [hidden_rows(firsts[0], FAR_ROWS[0], intra, qfeat, gate_input, gain, parts, [other_rest])]
    own.append(hidden_rows(firsts[1], FAR_ROWS[1], intra, qfeat, gate_input, gain, parts, own))
    other = [swap(own[0]), swap(own[1])]

    far_up, far_down, last = [], [], own[1]
    for i, n in enumerate(FAR_ROWS):
        far = (((0, 0, n, (), 0, 0), (0, n, n, (), 1, 0)),)
        top, bottom = project(
            "share_far", own[i : i + 1], other[i : i + 1], own_weight, other_far, ((0, 0),),
            far, [(n + PADDING[i], BF16)] * 2, after=[last], flops=(10**11, 1)[i],
        )
        far_up.append(up(top))
        far_down.append(down(bottom))
        last = top

    def both(part, terms, out):
        return tuple((i, part * n, n, terms(i), out, firsts[i]) for i, n in enumerate(FAR_ROWS))

    near_blocks = ((1, 0), (2, 1))
    near = tuple(both(part, lambda i: (), g) for g, part in ((0, 1), (1, 0)))
    up_share, down_share = project(
        "share_near", own, other, own_weight, other_rest, near_blocks, near, [(half, BF16)] * 2,
        after=[last],
    )
    up_share, down_share = settled([up_share, down_share], [far_up[0], far_down[0]])
    bottom_from_below, top_from_above = up(up_share), down(down_share)

    passing = tuple(both(part, lambda i: ((2 * g + i, 0),), g) for g, part in ((0, 0), (1, 1)))
    up_sum, down_sum = project(
        "share_passing", own, other, own_weight, other_rest, near_blocks, passing, [(half, BF16)] * 2,
        adds=[*far_up, *far_down], after=[up_share], flops=10**11,
    )
    top_from_below, bottom_from_above = up(up_sum), down(down_sum)

    home = (both(0, lambda i: ((0, firsts[i]),), 0) + both(1, lambda i: ((1, firsts[i]),), 1),)
    top, bottom = project(
        "share_own", own, other, own_weight, other_rest, ((3, 2),), home, [(half, F32)] * 2,
        adds=[top_from_above, bottom_from_below], after=[up_sum],
    )
    return finish(top, bottom, top_from_below, bottom_from_above)


def solution(mesh):
    return jax.shard_map(
        on_device,
        mesh=mesh,
        in_specs=(
            P("ctx", "tp"),
            P("ctx", "tp"),
            P("ctx", "tp"),
            P("ctx", "tp"),
            P("tp"),
            P("tp", None),
        ),
        out_specs=P("ctx", "tp"),
        check_vma=False,
    )
```

```python
import functools

import jax
import jax.numpy as jnp
from jax import lax
from jax.experimental import pallas as pl
from jax.experimental.pallas import tpu as pltpu
from jax.sharding import PartitionSpec as P

DH = 128
N_X = 4
N_Z = 4
N_Y = 4
CHUNK = 256
F32 = jnp.float32
BF16 = jnp.bfloat16
FAR_ROWS = (256, 256)
PADDING = (0, 0)
BLOCK_ORDER = (2, 1, 3, 0)


def shift_x(k):
    return [(z * N_X + x, z * N_X + (x + k) % N_X) for z in range(N_Z) for x in range(N_X)]


def later_z(k):
    return [(z * N_X + x, (z + k) * N_X + x) for z in range(N_Z - k) for x in range(N_X)]


def shift_y(k):
    return [(y * 2 + c, ((y + k) % N_Y) * 2 + c) for y in range(N_Y) for c in range(2)]


OTHER_CORE = [(i, i ^ 1) for i in range(2 * N_Y)]


def sigmoid(x):
    return 0.5 * jnp.tanh(0.5 * x) + 0.5


def feature(x):
    wide = x.astype(F32)
    return (wide * sigmoid(wide)).astype(BF16)


def call(kernel, vmem=16, flops=1, **kwargs):
    compiler_params = pltpu.CompilerParams(vmem_limit_bytes=vmem << 20)
    cost = pl.CostEstimate(flops=flops, bytes_accessed=1, transcendentals=0)
    return pl.pallas_call(kernel, compiler_params=compiler_params, cost_estimate=cost, **kwargs)


def in_hbm(x):
    return pltpu.with_memory_space_constraint(x, pltpu.HBM)


def in_vmem(x):
    return pltpu.with_memory_space_constraint(x, pltpu.VMEM)


IN_VMEM = pl.BlockSpec(memory_space=pltpu.VMEM)
ANYWHERE = pl.BlockSpec(memory_space=pl.ANY)


def state_kernel(k_ref, v_ref, state_ref):
    for h in range(k_ref.shape[1] // DH):
        cols = slice(h * DH, (h + 1) * DH)
        kf = feature(k_ref[:, cols])
        state = lax.dot_general(kf, v_ref[:, cols], (((0,), (0,)), ((), ())), preferred_element_type=F32)
        state_ref[cols, :] = state.astype(BF16)


def local_states(keys, values):
    rows, width = keys.shape
    block = 2 * DH
    spec = pl.BlockSpec((rows, block), lambda i: (0, i))
    return call(
        state_kernel,
        name="local_states",
        grid=(width // block,),
        in_specs=[spec, spec],
        out_specs=pl.BlockSpec((block, DH), lambda i: (i, 0)),
        out_shape=jax.ShapeDtypeStruct((width, DH), BF16),
    )(in_hbm(keys), in_hbm(values))


def split(x):
    high = x.astype(BF16)
    return high, (x - high.astype(F32)).astype(BF16)


def two_part_dot(q, high, low):
    return jnp.dot(
        jnp.concatenate([q, q], axis=1), jnp.concatenate([high, low], axis=0), preferred_element_type=F32
    )


def intra_kernel(q_ref, k_ref, v_ref, after_ref, intra_ref, qfeat_ref):
    rows, block = q_ref.shape
    t = lax.broadcasted_iota(jnp.int32, (CHUNK, CHUNK), 0)
    s = lax.broadcasted_iota(jnp.int32, (CHUNK, CHUNK), 1)
    causal = s <= t
    heads = range(block // DH)
    cols = [slice(h * DH, (h + 1) * DH) for h in heads]
    out_cols = [pl.ds(pl.multiple_of(pl.program_id(0) * block + h * DH, DH), DH) for h in heads]
    states = [jnp.zeros((DH, DH), F32) for _ in heads]
    for i in range(rows // CHUNK):
        here = slice(i * CHUNK, (i + 1) * CHUNK)
        q = [feature(q_ref[here, c]) for c in cols]
        k = [feature(k_ref[here, c]) for c in cols]
        v = [v_ref[here, c] for c in cols]
        scores = [
            lax.dot_general(q[h], k[h], (((1,), (1,)), ((), ())), preferred_element_type=F32) for h in heads
        ]
        before = [two_part_dot(q[h], *split(states[h])) for h in heads] if i else None
        if (i + 1) * CHUNK < rows:
            states = [
                states[h] + lax.dot_general(k[h], v[h], (((0,), (0,)), ((), ())), preferred_element_type=F32)
                for h in heads
            ]
        scores = [jnp.where(causal, x, 0.0).astype(BF16) for x in scores]
        out = [jnp.dot(scores[h], v[h], preferred_element_type=F32) for h in heads]
        for h in heads:
            qfeat_ref[here, out_cols[h]] = q[h]
            intra_ref[here, out_cols[h]] = out[h] + before[h] if i else out[h]


def intra_block(queries, keys, values, after):
    rows, width = keys.shape
    block = 4 * DH
    spec = pl.BlockSpec((rows, block), lambda i: (0, i))
    return call(
        intra_kernel,
        name="intra_block",
        vmem=28,
        flops=10**11,
        grid=(width // block,),
        in_specs=[spec] * 3 + [ANYWHERE],
        out_specs=[IN_VMEM] * 2,
        out_shape=[
            pltpu.VMEM((rows, width), F32),
            pltpu.VMEM((rows, width), BF16),
        ],
    )(in_hbm(queries), in_hbm(keys), in_hbm(values), *after)


def sort_columns_kernel(blocks_ref, weight_ref, after_ref, far_ref, rest_ref, mine_ref):
    step = pl.program_id(0)

    @pl.when(step == 0)
    def _():
        far_ref[0] = weight_ref[...]

    @pl.when((step > 0) & (step < N_Y))
    def _():
        rest_ref[0] = weight_ref[...]

    @pl.when(step >= N_Y)
    def _():
        mine_ref[0] = weight_ref[...]


def sort_columns(weight, theirs, mine, after):
    rows, width = weight.shape
    block = (rows, width // (2 * N_Y))
    return call(
        sort_columns_kernel,
        vmem=24,
        name="sort_columns",
        grid_spec=pltpu.PrefetchScalarGridSpec(
            num_scalar_prefetch=1,
            grid=(2 * N_Y,),
            in_specs=[pl.BlockSpec(block, lambda i, b: (0, b[i])), ANYWHERE],
            out_specs=[
                pl.BlockSpec((1, *block), lambda i, b: (0, 0, 0)),
                pl.BlockSpec((1, *block), lambda i, b: (jnp.clip(i - 1, 0, N_Y - 2), 0, 0)),
                pl.BlockSpec((1, *block), lambda i, b: (jnp.maximum(i - N_Y, 0), 0, 0)),
            ],
        ),
        out_shape=[pltpu.HBM((n, *block), BF16) for n in (1, N_Y - 1, N_Y)],
    )(jnp.stack(theirs + mine), in_hbm(weight), *after)


def pass_kernel(*refs):
    pass


def settled(arrays, after):
    return call(
        pass_kernel,
        name="settled",
        in_specs=[IN_VMEM] * len(arrays) + [ANYWHERE] * len(after),
        out_specs=[IN_VMEM] * len(arrays),
        out_shape=[pltpu.VMEM(a.shape, a.dtype) for a in arrays],
        input_output_aliases={i: i for i in range(len(arrays))},
    )(*map(in_vmem, arrays), *after)


def hidden_kernel(n_parts, first, rows, *refs):
    intra_ref, qfeat_ref, gate_ref, gain_ref = refs[:4]
    part_refs, hidden_ref, both_ref = refs[4 : 4 + n_parts], refs[-2], refs[-1]
    tokens, width = intra_ref.shape

    prefix = part_refs[0][...].astype(F32)
    for ref in part_refs[1:]:
        prefix += ref[...].astype(F32)
    high, low = split(prefix)
    for h in range(width // DH):
        both_ref[h, :DH, :] = high[h * DH : (h + 1) * DH]
        both_ref[h, DH:, :] = low[h * DH : (h + 1) * DH]

    for part in range(2):
        here = slice(part * tokens // 2 + first, part * tokens // 2 + first + rows)
        there = slice(part * rows, (part + 1) * rows)
        for h in range(width // DH):
            cols = slice(h * DH, (h + 1) * DH)
            q = qfeat_ref[here, cols]
            inter = jnp.dot(jnp.concatenate([q, q], axis=1), both_ref[h], preferred_element_type=F32)
            attn = intra_ref[here, cols] + inter
            scale = lax.rsqrt(jnp.mean(attn * attn, axis=-1, keepdims=True) + 1e-06)
            gate = sigmoid(gate_ref[here, cols].astype(F32))
            hidden_ref[there, cols] = (attn * scale * gain_ref[:, cols] * gate).astype(BF16)


def hidden_rows(first, rows, intra, qfeat, gate_input, gain, parts, after):
    width = intra.shape[1]
    return call(
        functools.partial(hidden_kernel, len(parts), first, rows),
        name="hidden_rows",
        in_specs=[IN_VMEM] * (4 + len(parts)) + [ANYWHERE] * len(after),
        out_specs=IN_VMEM,
        out_shape=pltpu.VMEM((2 * rows, width), BF16),
        scratch_shapes=[pltpu.VMEM((width // DH, 2 * DH, DH), BF16)],
    )(*map(in_vmem, [intra, qfeat, gate_input, gain, *parts]), *after)


def project_kernel(blocks, plan, n_hidden, n_adds, n_outs, *refs):
    own, other = refs[:n_hidden], refs[n_hidden : 2 * n_hidden]
    w_own, w_other = refs[2 * n_hidden : 2 * n_hidden + 2]
    adds = refs[2 * n_hidden + 2 :][:n_adds]
    outs = refs[len(refs) - n_outs :]
    step = outs[0].shape[1] // 3
    ends = [max(piece[5] + piece[2] for pieces in plan for piece in pieces if piece[4] == out) for out in range(n_outs)]
    for (mine, theirs), pieces in zip(blocks, plan):
        for source, first, rows, terms, out, at in pieces:

            def third(i, _, mine=mine, theirs=theirs, source=source, first=first, rows=rows, terms=terms, out=out, at=at):
                cols = pl.ds(pl.multiple_of(i * step, step), step)
                here = slice(first, first + rows)
                value = jnp.dot(own[source][here, :], w_own[mine, :, cols], preferred_element_type=F32)
                value += jnp.dot(other[source][here, :], w_other[theirs, :, cols], preferred_element_type=F32)
                for term, term_first in terms:
                    value += adds[term][term_first : term_first + rows, cols].astype(F32)
                outs[out][at : at + rows, cols] = value.astype(outs[out].dtype)
                return 0

            lax.fori_loop(0, 3, third, 0)
    for out, end in zip(outs, ends):
        if end < out.shape[0]:
            out[end:, :] = jnp.zeros((out.shape[0] - end, out.shape[1]), out.dtype)


def project(name, own, other, w_own, w_other, blocks, plan, outs, adds=(), after=(), flops=1):
    width = w_own.shape[2]
    operands = [*own, *other, w_own, w_other, *adds]
    return call(
        functools.partial(project_kernel, blocks, plan, len(own), len(adds), len(outs)),
        name=name,
        flops=flops,
        in_specs=[IN_VMEM] * len(operands) + [ANYWHERE] * len(after),
        out_specs=[IN_VMEM] * len(outs),
        out_shape=[pltpu.VMEM((n, width), dtype) for n, dtype in outs],
    )(*map(in_vmem, operands), *after)


def finish_kernel(value_ref, add_ref, *refs):
    out_ref = refs[-1]
    rows = out_ref.shape[0]
    here = pl.ds(pl.multiple_of(pl.program_id(0) * rows, rows), rows)
    out_ref[...] = (value_ref[here, :] + add_ref[here, :].astype(F32)).astype(BF16)


def finish(part, value, add, begun=()):
    rows, width = value.shape
    block = rows // 2
    return call(
        finish_kernel,
        name="finish",
        grid=(rows // block,),
        in_specs=[IN_VMEM] * 2 + [ANYWHERE] * len(begun),
        out_specs=pl.BlockSpec((block, width), lambda i: (part * (rows // block) + i, 0)),
        out_shape=jax.ShapeDtypeStruct((2 * rows, width), BF16),
        input_output_aliases={2: 0} if begun else {},
    )(in_vmem(value), in_vmem(add), *begun)


def on_device(queries, key_proj, values, gate_input, norm_gain, out_weight):
    rows, width = queries.shape
    half = rows // 2
    firsts = (0, FAR_ROWS[0])
    x = lax.rem(lax.axis_index("ctx"), N_X)
    y, core = lax.axis_index("tp") // 2, lax.rem(lax.axis_index("tp"), 2)
    gain = norm_gain[None, :]
    mine = [((y + k) % N_Y * 2 + core).astype(jnp.int32) for k in BLOCK_ORDER]
    theirs = [((y + k) % N_Y * 2 + 1 - core).astype(jnp.int32) for k in BLOCK_ORDER]

    state = local_states(key_proj, values)
    along_x = [lax.ppermute(state, "ctx", shift_x(k)) for k in (2, 3, 1)]
    theirs_far, theirs_rest, own_weight = sort_columns(out_weight, theirs, mine, [state])
    swap = lambda a: lax.ppermute(a, "tp", OTHER_CORE)
    other_far, other_rest = swap(theirs_far), swap(theirs_rest)
    state, own_weight = lax.optimization_barrier((state, own_weight))
    intra, qfeat = intra_block(queries, key_proj, values, [state])
    total = state.astype(F32)
    earlier = jnp.zeros_like(total)
    for k, part in zip((2, 3, 1), along_x):
        wide = part.astype(F32)
        total += wide
        earlier += jnp.where(k <= x, wide, 0.0)
    total = total.astype(BF16)
    along_z = [lax.ppermute(total, "ctx", later_z(k)) for k in (2, 3, 1)]
    parts = [earlier, *along_z]

    up = lambda a: lax.ppermute(a, "tp", shift_y(1))
    down = lambda a: lax.ppermute(a, "tp", shift_y(-1))
    own = [hidden_rows(firsts[0], FAR_ROWS[0], intra, qfeat, gate_input, gain, parts, [other_rest])]
    own.append(hidden_rows(firsts[1], FAR_ROWS[1], intra, qfeat, gate_input, gain, parts, own))
    other = [swap(own[0]), swap(own[1])]

    far_up, far_down, last = [], [], own[1]
    for i, n in enumerate(FAR_ROWS):
        far = (((0, 0, n, (), 0, 0), (0, n, n, (), 1, 0)),)
        top, bottom = project(
            "share_far", own[i : i + 1], other[i : i + 1], own_weight, other_far, ((0, 0),),
            far, [(n + PADDING[i], BF16)] * 2, after=[last], flops=(10**11, 1)[i],
        )
        far_up.append(up(top))
        far_down.append(down(bottom))
        last = top

    def both(part, terms, out):
        return tuple((i, part * n, n, terms(i), out, firsts[i]) for i, n in enumerate(FAR_ROWS))

    near_blocks = ((1, 0), (2, 1))
    near = tuple(both(part, lambda i: (), g) for g, part in ((0, 1), (1, 0)))
    up_share, down_share = project(
        "share_near", own, other, own_weight, other_rest, near_blocks, near, [(half, BF16)] * 2,
        after=[last],
    )
    up_share, down_share = settled([up_share, down_share], [far_up[0], far_down[0]])
    bottom_from_below, top_from_above = up(up_share), down(down_share)

    passing = tuple(both(part, lambda i: ((2 * g + i, 0),), g) for g, part in ((0, 0), (1, 1)))
    up_sum, down_sum = project(
        "share_passing", own, other, own_weight, other_rest, near_blocks, passing, [(half, BF16)] * 2,
        adds=[*far_up, *far_down], after=[up_share], flops=10**11,
    )
    top_from_below, bottom_from_above = up(up_sum), down(down_sum)

    home = (both(0, lambda i: ((0, firsts[i]),), 0) + both(1, lambda i: ((1, firsts[i]),), 1),)
    top, bottom = project(
        "share_own", own, other, own_weight, other_rest, ((3, 2),), home, [(half, F32)] * 2,
        adds=[top_from_above, bottom_from_below], after=[up_sum],
    )
    out = finish(1, bottom, bottom_from_above)
    return finish(0, top, top_from_below, [out])


def solution(mesh):
    return jax.shard_map(
        on_device,
        mesh=mesh,
        in_specs=(
            P("ctx", "tp"),
            P("ctx", "tp"),
            P("ctx", "tp"),
            P("ctx", "tp"),
            P("tp"),
            P("tp", None),
        ),
        out_specs=P("ctx", "tp"),
        check_vma=False,
    )
```

```python
import functools

import jax
import jax.numpy as jnp
from jax import lax
from jax.experimental import pallas as pl
from jax.experimental.pallas import tpu as pltpu
from jax.sharding import PartitionSpec as P

DH = 128
N_X = 4
N_Z = 4
N_Y = 4
CHUNK = 256
F32 = jnp.float32
BF16 = jnp.bfloat16
FAR_ROWS = (256, 256)
PADDING = (0, 0)
BLOCK_ORDER = (2, 1, 3, 0)


def shift_x(k):
    return [(z * N_X + x, z * N_X + (x + k) % N_X) for z in range(N_Z) for x in range(N_X)]


def later_z(k):
    return [(z * N_X + x, (z + k) * N_X + x) for z in range(N_Z - k) for x in range(N_X)]


def shift_y(k):
    return [(y * 2 + c, ((y + k) % N_Y) * 2 + c) for y in range(N_Y) for c in range(2)]


OTHER_CORE = [(i, i ^ 1) for i in range(2 * N_Y)]


def sigmoid(x):
    return 0.5 * jnp.tanh(0.5 * x) + 0.5


def feature(x):
    wide = x.astype(F32)
    return (wide * sigmoid(wide)).astype(BF16)


def call(kernel, vmem=16, flops=1, **kwargs):
    compiler_params = pltpu.CompilerParams(vmem_limit_bytes=vmem << 20)
    cost = pl.CostEstimate(flops=flops, bytes_accessed=1, transcendentals=0)
    return pl.pallas_call(kernel, compiler_params=compiler_params, cost_estimate=cost, **kwargs)


def in_hbm(x):
    return pltpu.with_memory_space_constraint(x, pltpu.HBM)


def in_vmem(x):
    return pltpu.with_memory_space_constraint(x, pltpu.VMEM)


IN_VMEM = pl.BlockSpec(memory_space=pltpu.VMEM)
ANYWHERE = pl.BlockSpec(memory_space=pl.ANY)


def state_kernel(k_ref, v_ref, state_ref):
    for h in range(k_ref.shape[1] // DH):
        cols = slice(h * DH, (h + 1) * DH)
        kf = feature(k_ref[:, cols])
        state = lax.dot_general(kf, v_ref[:, cols], (((0,), (0,)), ((), ())), preferred_element_type=F32)
        state_ref[cols, :] = state.astype(BF16)


def local_states(keys, values):
    rows, width = keys.shape
    block = 2 * DH
    spec = pl.BlockSpec((rows, block), lambda i: (0, i))
    return call(
        state_kernel,
        name="local_states",
        grid=(width // block,),
        in_specs=[spec, spec],
        out_specs=pl.BlockSpec((block, DH), lambda i: (i, 0)),
        out_shape=jax.ShapeDtypeStruct((width, DH), BF16),
    )(in_hbm(keys), in_hbm(values))


def split(x):
    high = x.astype(BF16)
    return high, (x - high.astype(F32)).astype(BF16)


def two_part_dot(q, high, low):
    return jnp.dot(
        jnp.concatenate([q, q], axis=1), jnp.concatenate([high, low], axis=0), preferred_element_type=F32
    )


def intra_kernel(q_ref, k_ref, v_ref, after_ref, intra_ref, qfeat_ref):
    rows, block = q_ref.shape
    t = lax.broadcasted_iota(jnp.int32, (CHUNK, CHUNK), 0)
    s = lax.broadcasted_iota(jnp.int32, (CHUNK, CHUNK), 1)
    causal = s <= t
    heads = range(block // DH)
    cols = [slice(h * DH, (h + 1) * DH) for h in heads]
    out_cols = [pl.ds(pl.multiple_of(pl.program_id(0) * block + h * DH, DH), DH) for h in heads]
    states = [jnp.zeros((DH, DH), F32) for _ in heads]
    for i in range(rows // CHUNK):
        here = slice(i * CHUNK, (i + 1) * CHUNK)
        q = [feature(q_ref[here, c]) for c in cols]
        k = [feature(k_ref[here, c]) for c in cols]
        v = [v_ref[here, c] for c in cols]
        scores = [
            lax.dot_general(q[h], k[h], (((1,), (1,)), ((), ())), preferred_element_type=F32) for h in heads
        ]
        before = [two_part_dot(q[h], *split(states[h])) for h in heads] if i else None
        if (i + 1) * CHUNK < rows:
            states = [
                states[h] + lax.dot_general(k[h], v[h], (((0,), (0,)), ((), ())), preferred_element_type=F32)
                for h in heads
            ]
        scores = [jnp.where(causal, x, 0.0).astype(BF16) for x in scores]
        out = [jnp.dot(scores[h], v[h], preferred_element_type=F32) for h in heads]
        for h in heads:
            qfeat_ref[here, out_cols[h]] = q[h]
            intra_ref[here, out_cols[h]] = out[h] + before[h] if i else out[h]


def intra_block(queries, keys, values, after):
    rows, width = keys.shape
    block = 4 * DH
    spec = pl.BlockSpec((rows, block), lambda i: (0, i))
    return call(
        intra_kernel,
        name="intra_block",
        vmem=28,
        flops=10**11,
        grid=(width // block,),
        in_specs=[spec] * 3 + [ANYWHERE],
        out_specs=[IN_VMEM] * 2,
        out_shape=[
            pltpu.VMEM((rows, width), F32),
            pltpu.VMEM((rows, width), BF16),
        ],
    )(in_hbm(queries), in_hbm(keys), in_hbm(values), *after)


def sort_columns_kernel(blocks_ref, weight_ref, after_ref, far_ref, rest_ref, mine_ref):
    step = pl.program_id(0)

    @pl.when(step == 0)
    def _():
        far_ref[0] = weight_ref[...]

    @pl.when((step > 0) & (step < N_Y))
    def _():
        rest_ref[0] = weight_ref[...]

    @pl.when(step >= N_Y)
    def _():
        mine_ref[0] = weight_ref[...]


def sort_columns(weight, theirs, mine, after):
    rows, width = weight.shape
    block = (rows, width // (2 * N_Y))
    return call(
        sort_columns_kernel,
        vmem=24,
        name="sort_columns",
        grid_spec=pltpu.PrefetchScalarGridSpec(
            num_scalar_prefetch=1,
            grid=(2 * N_Y,),
            in_specs=[pl.BlockSpec(block, lambda i, b: (0, b[i])), ANYWHERE],
            out_specs=[
                pl.BlockSpec((1, *block), lambda i, b: (0, 0, 0)),
                pl.BlockSpec((1, *block), lambda i, b: (jnp.clip(i - 1, 0, N_Y - 2), 0, 0)),
                pl.BlockSpec((1, *block), lambda i, b: (jnp.maximum(i - N_Y, 0), 0, 0)),
            ],
        ),
        out_shape=[pltpu.HBM((n, *block), BF16) for n in (1, N_Y - 1, N_Y)],
    )(jnp.stack(theirs + mine), in_hbm(weight), *after)


def pass_kernel(*refs):
    pass


def settled(arrays, after):
    return call(
        pass_kernel,
        name="settled",
        in_specs=[IN_VMEM] * len(arrays) + [ANYWHERE] * len(after),
        out_specs=[IN_VMEM] * len(arrays),
        out_shape=[pltpu.VMEM(a.shape, a.dtype) for a in arrays],
        input_output_aliases={i: i for i in range(len(arrays))},
    )(*map(in_vmem, arrays), *after)


def hidden_kernel(n_parts, first, rows, *refs):
    intra_ref, qfeat_ref, gate_ref, gain_ref = refs[:4]
    part_refs, hidden_ref, both_ref = refs[4 : 4 + n_parts], refs[-2], refs[-1]
    tokens, width = intra_ref.shape

    prefix = part_refs[0][...].astype(F32)
    for ref in part_refs[1:]:
        prefix += ref[...].astype(F32)
    high, low = split(prefix)
    for h in range(width // DH):
        both_ref[h, :DH, :] = high[h * DH : (h + 1) * DH]
        both_ref[h, DH:, :] = low[h * DH : (h + 1) * DH]

    for part in range(2):
        here = slice(part * tokens // 2 + first, part * tokens // 2 + first + rows)
        there = slice(part * rows, (part + 1) * rows)
        for h in range(width // DH):
            cols = slice(h * DH, (h + 1) * DH)
            q = qfeat_ref[here, cols]
            inter = jnp.dot(jnp.concatenate([q, q], axis=1), both_ref[h], preferred_element_type=F32)
            attn = intra_ref[here, cols] + inter
            scale = lax.rsqrt(jnp.mean(attn * attn, axis=-1, keepdims=True) + 1e-06)
            gate = sigmoid(gate_ref[here, cols].astype(F32))
            hidden_ref[there, cols] = (attn * scale * gain_ref[:, cols] * gate).astype(BF16)


def hidden_rows(first, rows, intra, qfeat, gate_input, gain, parts, after):
    width = intra.shape[1]
    return call(
        functools.partial(hidden_kernel, len(parts), first, rows),
        name="hidden_rows",
        in_specs=[IN_VMEM] * (4 + len(parts)) + [ANYWHERE] * len(after),
        out_specs=IN_VMEM,
        out_shape=pltpu.VMEM((2 * rows, width), BF16),
        scratch_shapes=[pltpu.VMEM((width // DH, 2 * DH, DH), BF16)],
    )(*map(in_vmem, [intra, qfeat, gate_input, gain, *parts]), *after)


def project_kernel(blocks, plan, n_hidden, n_adds, n_outs, *refs):
    own, other = refs[:n_hidden], refs[n_hidden : 2 * n_hidden]
    w_own, w_other = refs[2 * n_hidden : 2 * n_hidden + 2]
    adds = refs[2 * n_hidden + 2 :][:n_adds]
    outs = refs[len(refs) - n_outs :]
    step = outs[0].shape[1] // 3
    ends = [max(piece[5] + piece[2] for pieces in plan for piece in pieces if piece[4] == out) for out in range(n_outs)]
    for (mine, theirs), pieces in zip(blocks, plan):
        for source, first, rows, terms, out, at in pieces:

            def third(i, _, mine=mine, theirs=theirs, source=source, first=first, rows=rows, terms=terms, out=out, at=at):
                cols = pl.ds(pl.multiple_of(i * step, step), step)
                here = slice(first, first + rows)
                value = jnp.dot(own[source][here, :], w_own[mine, :, cols], preferred_element_type=F32)
                value += jnp.dot(other[source][here, :], w_other[theirs, :, cols], preferred_element_type=F32)
                for term, term_first in terms:
                    value += adds[term][term_first : term_first + rows, cols].astype(F32)
                outs[out][at : at + rows, cols] = value.astype(outs[out].dtype)
                return 0

            lax.fori_loop(0, 3, third, 0)
    for out, end in zip(outs, ends):
        if end < out.shape[0]:
            out[end:, :] = jnp.zeros((out.shape[0] - end, out.shape[1]), out.dtype)


def project(name, own, other, w_own, w_other, blocks, plan, outs, adds=(), after=(), flops=1):
    width = w_own.shape[2]
    operands = [*own, *other, w_own, w_other, *adds]
    return call(
        functools.partial(project_kernel, blocks, plan, len(own), len(adds), len(outs)),
        name=name,
        flops=flops,
        in_specs=[IN_VMEM] * len(operands) + [ANYWHERE] * len(after),
        out_specs=[IN_VMEM] * len(outs),
        out_shape=[pltpu.VMEM((n, width), dtype) for n, dtype in outs],
    )(*map(in_vmem, operands), *after)


def finish_kernel(value_ref, add_ref, *refs):
    out_ref = refs[-1]
    rows = out_ref.shape[0]
    here = pl.ds(pl.multiple_of(pl.program_id(0) * rows, rows), rows)
    out_ref[...] = (value_ref[here, :] + add_ref[here, :].astype(F32)).astype(BF16)


def finish(part, value, add, begun=()):
    rows, width = value.shape
    block = rows // 4
    return call(
        finish_kernel,
        name="finish",
        grid=(rows // block,),
        in_specs=[IN_VMEM] * 2 + [ANYWHERE] * len(begun),
        out_specs=pl.BlockSpec((block, width), lambda i: (part * (rows // block) + i, 0)),
        out_shape=jax.ShapeDtypeStruct((2 * rows, width), BF16),
        input_output_aliases={2: 0} if begun else {},
    )(in_vmem(value), in_vmem(add), *begun)


def on_device(queries, key_proj, values, gate_input, norm_gain, out_weight):
    rows, width = queries.shape
    half = rows // 2
    firsts = (0, FAR_ROWS[0])
    x = lax.rem(lax.axis_index("ctx"), N_X)
    y, core = lax.axis_index("tp") // 2, lax.rem(lax.axis_index("tp"), 2)
    gain = norm_gain[None, :]
    mine = [((y + k) % N_Y * 2 + core).astype(jnp.int32) for k in BLOCK_ORDER]
    theirs = [((y + k) % N_Y * 2 + 1 - core).astype(jnp.int32) for k in BLOCK_ORDER]

    state = local_states(key_proj, values)
    along_x = [lax.ppermute(state, "ctx", shift_x(k)) for k in (2, 3, 1)]
    theirs_far, theirs_rest, own_weight = sort_columns(out_weight, theirs, mine, [state])
    swap = lambda a: lax.ppermute(a, "tp", OTHER_CORE)
    other_far, other_rest = swap(theirs_far), swap(theirs_rest)
    state, own_weight = lax.optimization_barrier((state, own_weight))
    intra, qfeat = intra_block(queries, key_proj, values, [state])
    total = state.astype(F32)
    earlier = jnp.zeros_like(total)
    for k, part in zip((2, 3, 1), along_x):
        wide = part.astype(F32)
        total += wide
        earlier += jnp.where(k <= x, wide, 0.0)
    total = total.astype(BF16)
    along_z = [lax.ppermute(total, "ctx", later_z(k)) for k in (3, 2, 1)]
    parts = [earlier, *along_z]

    up = lambda a: lax.ppermute(a, "tp", shift_y(1))
    down = lambda a: lax.ppermute(a, "tp", shift_y(-1))
    own = [hidden_rows(firsts[0], FAR_ROWS[0], intra, qfeat, gate_input, gain, parts, [other_rest])]
    own.append(hidden_rows(firsts[1], FAR_ROWS[1], intra, qfeat, gate_input, gain, parts, own))
    other = [swap(own[0]), swap(own[1])]

    far_up, far_down, last = [], [], own[1]
    for i, n in enumerate(FAR_ROWS):
        far = (((0, 0, n, (), 0, 0), (0, n, n, (), 1, 0)),)
        top, bottom = project(
            "share_far", own[i : i + 1], other[i : i + 1], own_weight, other_far, ((0, 0),),
            far, [(n + PADDING[i], BF16)] * 2, after=[last], flops=(10**11, 1)[i],
        )
        far_up.append(up(top))
        far_down.append(down(bottom))
        last = top

    def both(part, terms, out):
        return tuple((i, part * n, n, terms(i), out, firsts[i]) for i, n in enumerate(FAR_ROWS))

    near_blocks = ((1, 0), (2, 1))
    near = tuple(both(part, lambda i: (), g) for g, part in ((0, 1), (1, 0)))
    up_share, down_share = project(
        "share_near", own, other, own_weight, other_rest, near_blocks, near, [(half, BF16)] * 2,
        after=[last],
    )
    up_share, down_share = settled([up_share, down_share], [far_up[0], far_down[0]])
    bottom_from_below, top_from_above = up(up_share), down(down_share)

    passing = tuple(both(part, lambda i: ((2 * g + i, 0),), g) for g, part in ((0, 0), (1, 1)))
    up_sum, down_sum = project(
        "share_passing", own, other, own_weight, other_rest, near_blocks, passing, [(half, BF16)] * 2,
        adds=[*far_up, *far_down], after=[up_share], flops=10**11,
    )
    top_from_below, bottom_from_above = up(up_sum), down(down_sum)

    home = (both(0, lambda i: ((0, firsts[i]),), 0) + both(1, lambda i: ((1, firsts[i]),), 1),)
    top, bottom = project(
        "share_own", own, other, own_weight, other_rest, ((3, 2),), home, [(half, F32)] * 2,
        adds=[top_from_above, bottom_from_below], after=[up_sum],
    )
    out = finish(1, bottom, bottom_from_above)
    return finish(0, top, top_from_below, [out])


def solution(mesh):
    return jax.shard_map(
        on_device,
        mesh=mesh,
        in_specs=(
            P("ctx", "tp"),
            P("ctx", "tp"),
            P("ctx", "tp"),
            P("ctx", "tp"),
            P("tp"),
            P("tp", None),
        ),
        out_specs=P("ctx", "tp"),
        check_vma=False,
    )
```

```python
import functools

import jax
import jax.numpy as jnp
from jax import lax
from jax.experimental import pallas as pl
from jax.experimental.pallas import tpu as pltpu
from jax.sharding import PartitionSpec as P

DH = 128
N_X = 4
N_Z = 4
N_Y = 4
CHUNK = 256
F32 = jnp.float32
BF16 = jnp.bfloat16
FAR_ROWS = (256, 256)
PADDING = (0, 0)
BLOCK_ORDER = (2, 1, 3, 0)


def shift_x(k):
    return [(z * N_X + x, z * N_X + (x + k) % N_X) for z in range(N_Z) for x in range(N_X)]


def later_z(k):
    return [(z * N_X + x, (z + k) * N_X + x) for z in range(N_Z - k) for x in range(N_X)]


def shift_y(k):
    return [(y * 2 + c, ((y + k) % N_Y) * 2 + c) for y in range(N_Y) for c in range(2)]


OTHER_CORE = [(i, i ^ 1) for i in range(2 * N_Y)]


def sigmoid(x):
    return 0.5 * jnp.tanh(0.5 * x) + 0.5


def feature(x):
    wide = x.astype(F32)
    return (wide * sigmoid(wide)).astype(BF16)


def call(kernel, vmem=16, flops=1, **kwargs):
    compiler_params = pltpu.CompilerParams(vmem_limit_bytes=vmem << 20)
    cost = pl.CostEstimate(flops=flops, bytes_accessed=1, transcendentals=0)
    return pl.pallas_call(kernel, compiler_params=compiler_params, cost_estimate=cost, **kwargs)


def in_hbm(x):
    return pltpu.with_memory_space_constraint(x, pltpu.HBM)


def in_vmem(x):
    return pltpu.with_memory_space_constraint(x, pltpu.VMEM)


IN_VMEM = pl.BlockSpec(memory_space=pltpu.VMEM)
ANYWHERE = pl.BlockSpec(memory_space=pl.ANY)


def state_kernel(k_ref, v_ref, state_ref):
    for h in range(k_ref.shape[1] // DH):
        cols = slice(h * DH, (h + 1) * DH)
        kf = feature(k_ref[:, cols])
        state = lax.dot_general(kf, v_ref[:, cols], (((0,), (0,)), ((), ())), preferred_element_type=F32)
        state_ref[cols, :] = state.astype(BF16)


def local_states(keys, values):
    rows, width = keys.shape
    block = 2 * DH
    spec = pl.BlockSpec((rows, block), lambda i: (0, i))
    return call(
        state_kernel,
        name="local_states",
        grid=(width // block,),
        in_specs=[spec, spec],
        out_specs=pl.BlockSpec((block, DH), lambda i: (i, 0)),
        out_shape=jax.ShapeDtypeStruct((width, DH), BF16),
    )(in_hbm(keys), in_hbm(values))


def split(x):
    high = x.astype(BF16)
    return high, (x - high.astype(F32)).astype(BF16)


def two_part_dot(q, high, low):
    return jnp.dot(
        jnp.concatenate([q, q], axis=1), jnp.concatenate([high, low], axis=0), preferred_element_type=F32
    )


def intra_kernel(q_ref, k_ref, v_ref, after_ref, intra_ref, qfeat_ref):
    rows, block = q_ref.shape
    t = lax.broadcasted_iota(jnp.int32, (CHUNK, CHUNK), 0)
    s = lax.broadcasted_iota(jnp.int32, (CHUNK, CHUNK), 1)
    causal = s <= t
    heads = range(block // DH)
    cols = [slice(h * DH, (h + 1) * DH) for h in heads]
    out_cols = [pl.ds(pl.multiple_of(pl.program_id(0) * block + h * DH, DH), DH) for h in heads]
    states = [jnp.zeros((DH, DH), F32) for _ in heads]
    for i in range(rows // CHUNK):
        here = slice(i * CHUNK, (i + 1) * CHUNK)
        q = [feature(q_ref[here, c]) for c in cols]
        k = [feature(k_ref[here, c]) for c in cols]
        v = [v_ref[here, c] for c in cols]
        scores = [
            lax.dot_general(q[h], k[h], (((1,), (1,)), ((), ())), preferred_element_type=F32) for h in heads
        ]
        before = [two_part_dot(q[h], *split(states[h])) for h in heads] if i else None
        if (i + 1) * CHUNK < rows:
            states = [
                states[h] + lax.dot_general(k[h], v[h], (((0,), (0,)), ((), ())), preferred_element_type=F32)
                for h in heads
            ]
        scores = [jnp.where(causal, x, 0.0).astype(BF16) for x in scores]
        out = [jnp.dot(scores[h], v[h], preferred_element_type=F32) for h in heads]
        for h in heads:
            qfeat_ref[here, out_cols[h]] = q[h]
            intra_ref[here, out_cols[h]] = out[h] + before[h] if i else out[h]


def intra_block(queries, keys, values, after):
    rows, width = keys.shape
    block = 4 * DH
    spec = pl.BlockSpec((rows, block), lambda i: (0, i))
    return call(
        intra_kernel,
        name="intra_block",
        vmem=28,
        flops=10**11,
        grid=(width // block,),
        in_specs=[spec] * 3 + [ANYWHERE],
        out_specs=[IN_VMEM] * 2,
        out_shape=[
            pltpu.VMEM((rows, width), F32),
            pltpu.VMEM((rows, width), BF16),
        ],
    )(in_hbm(queries), in_hbm(keys), in_hbm(values), *after)


def sort_columns_kernel(blocks_ref, weight_ref, after_ref, far_ref, rest_ref, mine_ref):
    step = pl.program_id(0)

    @pl.when(step == 0)
    def _():
        far_ref[0] = weight_ref[...]

    @pl.when((step > 0) & (step < N_Y))
    def _():
        rest_ref[0] = weight_ref[...]

    @pl.when(step >= N_Y)
    def _():
        mine_ref[0] = weight_ref[...]


def sort_columns(weight, theirs, mine, after):
    rows, width = weight.shape
    block = (rows, width // (2 * N_Y))
    return call(
        sort_columns_kernel,
        vmem=24,
        name="sort_columns",
        grid_spec=pltpu.PrefetchScalarGridSpec(
            num_scalar_prefetch=1,
            grid=(2 * N_Y,),
            in_specs=[pl.BlockSpec(block, lambda i, b: (0, b[i])), ANYWHERE],
            out_specs=[
                pl.BlockSpec((1, *block), lambda i, b: (0, 0, 0)),
                pl.BlockSpec((1, *block), lambda i, b: (jnp.clip(i - 1, 0, N_Y - 2), 0, 0)),
                pl.BlockSpec((1, *block), lambda i, b: (jnp.maximum(i - N_Y, 0), 0, 0)),
            ],
        ),
        out_shape=[pltpu.HBM((n, *block), BF16) for n in (1, N_Y - 1, N_Y)],
    )(jnp.stack(theirs + mine), in_hbm(weight), *after)


def pass_kernel(*refs):
    pass


def settled(arrays, after):
    return call(
        pass_kernel,
        name="settled",
        in_specs=[IN_VMEM] * len(arrays) + [ANYWHERE] * len(after),
        out_specs=[IN_VMEM] * len(arrays),
        out_shape=[pltpu.VMEM(a.shape, a.dtype) for a in arrays],
        input_output_aliases={i: i for i in range(len(arrays))},
    )(*map(in_vmem, arrays), *after)


def hidden_kernel(n_parts, first, rows, *refs):
    intra_ref, qfeat_ref, gate_ref, gain_ref = refs[:4]
    part_refs, hidden_ref, both_ref = refs[4 : 4 + n_parts], refs[-2], refs[-1]
    tokens, width = intra_ref.shape

    prefix = part_refs[0][...].astype(F32)
    for ref in part_refs[1:]:
        prefix += ref[...].astype(F32)
    high, low = split(prefix)
    for h in range(width // DH):
        both_ref[h, :DH, :] = high[h * DH : (h + 1) * DH]
        both_ref[h, DH:, :] = low[h * DH : (h + 1) * DH]

    for part in range(2):
        here = slice(part * tokens // 2 + first, part * tokens // 2 + first + rows)
        there = slice(part * rows, (part + 1) * rows)
        for h in range(width // DH):
            cols = slice(h * DH, (h + 1) * DH)
            q = qfeat_ref[here, cols]
            inter = jnp.dot(jnp.concatenate([q, q], axis=1), both_ref[h], preferred_element_type=F32)
            attn = intra_ref[here, cols] + inter
            scale = lax.rsqrt(jnp.mean(attn * attn, axis=-1, keepdims=True) + 1e-06)
            gate = sigmoid(gate_ref[here, cols].astype(F32))
            hidden_ref[there, cols] = (attn * scale * gain_ref[:, cols] * gate).astype(BF16)


def hidden_rows(first, rows, intra, qfeat, gate_input, gain, parts, after):
    width = intra.shape[1]
    return call(
        functools.partial(hidden_kernel, len(parts), first, rows),
        name="hidden_rows",
        in_specs=[IN_VMEM] * (4 + len(parts)) + [ANYWHERE] * len(after),
        out_specs=IN_VMEM,
        out_shape=pltpu.VMEM((2 * rows, width), BF16),
        scratch_shapes=[pltpu.VMEM((width // DH, 2 * DH, DH), BF16)],
    )(*map(in_vmem, [intra, qfeat, gate_input, gain, *parts]), *after)


def project_kernel(blocks, plan, n_hidden, n_adds, n_outs, *refs):
    own, other = refs[:n_hidden], refs[n_hidden : 2 * n_hidden]
    w_own, w_other = refs[2 * n_hidden : 2 * n_hidden + 2]
    adds = refs[2 * n_hidden + 2 :][:n_adds]
    outs = refs[len(refs) - n_outs :]
    step = outs[0].shape[1] // 3
    ends = [max(piece[5] + piece[2] for pieces in plan for piece in pieces if piece[4] == out) for out in range(n_outs)]
    for (mine, theirs), pieces in zip(blocks, plan):
        for source, first, rows, terms, out, at in pieces:

            def third(i, _, mine=mine, theirs=theirs, source=source, first=first, rows=rows, terms=terms, out=out, at=at):
                cols = pl.ds(pl.multiple_of(i * step, step), step)
                here = slice(first, first + rows)
                value = jnp.dot(own[source][here, :], w_own[mine, :, cols], preferred_element_type=F32)
                value += jnp.dot(other[source][here, :], w_other[theirs, :, cols], preferred_element_type=F32)
                for term, term_first in terms:
                    value += adds[term][term_first : term_first + rows, cols].astype(F32)
                outs[out][at : at + rows, cols] = value.astype(outs[out].dtype)
                return 0

            lax.fori_loop(0, 3, third, 0)
    for out, end in zip(outs, ends):
        if end < out.shape[0]:
            out[end:, :] = jnp.zeros((out.shape[0] - end, out.shape[1]), out.dtype)


def project(name, own, other, w_own, w_other, blocks, plan, outs, adds=(), after=(), flops=1):
    width = w_own.shape[2]
    operands = [*own, *other, w_own, w_other, *adds]
    return call(
        functools.partial(project_kernel, blocks, plan, len(own), len(adds), len(outs)),
        name=name,
        flops=flops,
        in_specs=[IN_VMEM] * len(operands) + [ANYWHERE] * len(after),
        out_specs=[IN_VMEM] * len(outs),
        out_shape=[pltpu.VMEM((n, width), dtype) for n, dtype in outs],
    )(*map(in_vmem, operands), *after)


def finish_kernel(value_ref, add_ref, *refs):
    out_ref = refs[-1]
    rows = out_ref.shape[0]
    here = pl.ds(pl.multiple_of(pl.program_id(0) * rows, rows), rows)
    out_ref[...] = (value_ref[here, :] + add_ref[here, :].astype(F32)).astype(BF16)


def finish(part, value, add, begun=()):
    rows, width = value.shape
    block = rows
    return call(
        finish_kernel,
        name="finish",
        grid=(rows // block,),
        in_specs=[IN_VMEM] * 2 + [ANYWHERE] * len(begun),
        out_specs=pl.BlockSpec((block, width), lambda i: (part * (rows // block) + i, 0)),
        out_shape=jax.ShapeDtypeStruct((2 * rows, width), BF16),
        input_output_aliases={2: 0} if begun else {},
    )(in_vmem(value), in_vmem(add), *begun)


def on_device(queries, key_proj, values, gate_input, norm_gain, out_weight):
    rows, width = queries.shape
    half = rows // 2
    firsts = (0, FAR_ROWS[0])
    x = lax.rem(lax.axis_index("ctx"), N_X)
    y, core = lax.axis_index("tp") // 2, lax.rem(lax.axis_index("tp"), 2)
    gain = norm_gain[None, :]
    mine = [((y + k) % N_Y * 2 + core).astype(jnp.int32) for k in BLOCK_ORDER]
    theirs = [((y + k) % N_Y * 2 + 1 - core).astype(jnp.int32) for k in BLOCK_ORDER]

    state = local_states(key_proj, values)
    along_x = [lax.ppermute(state, "ctx", shift_x(k)) for k in (2, 3, 1)]
    theirs_far, theirs_rest, own_weight = sort_columns(out_weight, theirs, mine, [state])
    swap = lambda a: lax.ppermute(a, "tp", OTHER_CORE)
    other_far, other_rest = swap(theirs_far), swap(theirs_rest)
    state, own_weight = lax.optimization_barrier((state, own_weight))
    intra, qfeat = intra_block(queries, key_proj, values, [state])
    total = state.astype(F32)
    earlier = jnp.zeros_like(total)
    for k, part in zip((2, 3, 1), along_x):
        wide = part.astype(F32)
        total += wide
        earlier += jnp.where(k <= x, wide, 0.0)
    total = total.astype(BF16)
    along_z = [lax.ppermute(total, "ctx", later_z(k)) for k in (2, 3, 1)]
    parts = [earlier, *along_z]

    up = lambda a: lax.ppermute(a, "tp", shift_y(1))
    down = lambda a: lax.ppermute(a, "tp", shift_y(-1))
    own = [hidden_rows(firsts[0], FAR_ROWS[0], intra, qfeat, gate_input, gain, parts, [other_rest])]
    own.append(hidden_rows(firsts[1], FAR_ROWS[1], intra, qfeat, gate_input, gain, parts, own))
    other = [swap(own[0]), swap(own[1])]

    far_up, far_down, last = [], [], own[1]
    for i, n in enumerate(FAR_ROWS):
        far = (((0, 0, n, (), 0, 0), (0, n, n, (), 1, 0)),)
        top, bottom = project(
            "share_far", own[i : i + 1], other[i : i + 1], own_weight, other_far, ((0, 0),),
            far, [(n + PADDING[i], BF16)] * 2, after=[last], flops=(10**11, 1)[i],
        )
        far_up.append(up(top))
        far_down.append(down(bottom))
        last = top

    def both(part, terms, out):
        return tuple((i, part * n, n, terms(i), out, firsts[i]) for i, n in enumerate(FAR_ROWS))

    near_blocks = ((1, 0), (2, 1))
    near = tuple(both(part, lambda i: (), g) for g, part in ((0, 1), (1, 0)))
    up_share, down_share = project(
        "share_near", own, other, own_weight, other_rest, near_blocks, near, [(half, BF16)] * 2,
        after=[last],
    )
    up_share, down_share = settled([up_share, down_share], [far_up[0], far_down[0]])
    bottom_from_below, top_from_above = up(up_share), down(down_share)

    passing = tuple(both(part, lambda i: ((2 * g + i, 0),), g) for g, part in ((0, 0), (1, 1)))
    up_sum, down_sum = project(
        "share_passing", own, other, own_weight, other_rest, near_blocks, passing, [(half, BF16)] * 2,
        adds=[*far_up, *far_down], after=[up_share], flops=10**11,
    )
    top_from_below, bottom_from_above = up(up_sum), down(down_sum)

    home = (both(0, lambda i: ((0, firsts[i]),), 0) + both(1, lambda i: ((1, firsts[i]),), 1),)
    top, bottom = project(
        "share_own", own, other, own_weight, other_rest, ((3, 2),), home, [(half, F32)] * 2,
        adds=[top_from_above, bottom_from_below], after=[up_sum],
    )
    out = finish(1, bottom, bottom_from_above)
    return finish(0, top, top_from_below, [out])


def solution(mesh):
    return jax.shard_map(
        on_device,
        mesh=mesh,
        in_specs=(
            P("ctx", "tp"),
            P("ctx", "tp"),
            P("ctx", "tp"),
            P("ctx", "tp"),
            P("tp"),
            P("tp", None),
        ),
        out_specs=P("ctx", "tp"),
        check_vma=False,
    )
```
